32 devices in a mesh: grp: 2 (over y), wide: 16 (over z, x, core).
Axes of the slice: x: 2, y: 2, z: 4, core: 2. Of those that a mesh axis runs over, the one named last changes fastest.
Arguments:
- year_slab: bfloat16 [1024, 4096], P(('grp', 'wide')), parts along dimension 0, may hold values from -12 to 12
- harmonic_fit: float32 [21, 4096], P(None, 'wide'), may hold values from -6 to 6
- patterns: bfloat16 [4096, 256], P('wide'), may hold values from -0.09375 to 0.09375
- reader_table: int32 [16], replicated, may hold values from 0 to 15, each once
- land_mask: int32 [4096], P('wide'), may hold values 0 or 1
Outputs:
- components: float32 [1024, 256], P(('grp', 'wide')), parts along dimension 0
The draws below stay inside these ranges and needn't reach their ends.
There are 2 independent parts, one for each index of `grp`. The reference program is written for one: setup_inputs(seed, part) draws one part's arguments, and reference() takes and returns one part's arrays. A program takes and returns all parts, laid end to end along the dimension named above; an argument that names none is the same for every part. Nothing has to cross between parts.
Inputs may be any that keep to these rules, and one draw needn't show every extreme that they name: `reader_table`: each of the 16 groups is held by exactly one reader.
All inputs are finite; a program needn't handle non-finite values. No bound on the sum of `land_mask` on one device may be relied on, other than what follows from the above.
Results may differ from the reference program's by a relative error of at most 0.0029.
Values may be sent and summed in bfloat16 or wider, within the bound.
A program may use at most 64 MiB of HBM per device.

```python
import math
import jax
import jax.numpy as jnp
from jax import lax

TCH = 32
K = 256
NHARM = 8
NDIUR = 2
NCOEF = 21
NCHUNK = 16
HOURS = 512
P_SIZE = 4096


def touch_ends(drawn, key, low, top_value):
    extent = drawn.shape
    index_at = [jax.random.randint(jax.random.fold_in(key, axis), (), 0, extent[axis]) for axis in range(len(extent))]
    drawn = drawn.at[tuple(index_at)].set(low)
    longest = extent.index(max(extent))
    index_at[longest] = (index_at[longest] + 1) % extent[longest]
    return drawn.at[tuple(index_at)].set(top_value)


def levels(stream_key, extent, shards, least, high):
    level = 1.0
    for position, shards_of in shards:
        heights = jax.random.uniform(jax.random.fold_in(jax.random.fold_in(stream_key, 6), position), (shards_of,), jnp.float32, least / len(shards), high / len(shards))
        level = level * jnp.repeat(jnp.exp(heights), extent[position] // shards_of).reshape((-1,) + (1,) * (len(extent) - 1 - position))
    return level


def noise(own_key, dims, spread, reach, shards=(), kind=jnp.bfloat16):
    values = jax.random.normal(own_key, dims, jnp.float32) * spread
    if len(shards) > 0:
        values = levels(own_key, dims, shards, -0.22, 0.18) * values
    return jnp.clip(values, min=-reach, max=reach).astype(kind)


def setup_inputs(seed: int = 0, part: int = 0) -> dict:
    key_of = jax.random.split(jax.random.key(seed), 6)
    part_splits = jax.random.split(jax.random.fold_in(key_of[5], part), 6)
    year_slab = noise(part_splits[0], (HOURS, P_SIZE), 2.0, 12.0, ((0, 16),))
    harmonic_fit = noise(key_of[1], (NCOEF, P_SIZE), 1.0, 6.0, ((1, 16),), jnp.float32)
    patterns = noise(key_of[2], (P_SIZE, K), P_SIZE ** -0.5, 0.09375, ((0, 16),))
    reader_table = jax.random.permutation(key_of[3], NCHUNK).astype(jnp.int32)
    land_mask = touch_ends((jax.random.randint(key_of[4], (P_SIZE,), 0, 10) < 3).astype(jnp.int32), jax.random.fold_in(key_of[4], 1), 0, 1)
    return dict(year_slab=year_slab, harmonic_fit=harmonic_fit, patterns=patterns, reader_table=reader_table, land_mask=land_mask)


def regressors(hours, period):
    orders = jnp.arange(1, NHARM + 1, dtype=jnp.int32)
    slow = ((hours[..., None] * orders) % period).astype(jnp.float32) * (2.0 * math.pi / period)
    daily_orders = jnp.arange(1, NDIUR + 1, dtype=jnp.int32)
    daily = ((hours[..., None] * daily_orders) % 24).astype(jnp.float32) * (2.0 * math.pi / 24.0)
    ones = jnp.ones(hours.shape + (1,), jnp.float32)
    return jnp.concatenate([ones, jnp.cos(slow), jnp.sin(slow), jnp.cos(daily), jnp.sin(daily)], -1)


def effective(harmonic_fit, land_mask):
    split = 1 + 2 * NHARM
    land = land_mask.astype(jnp.float32)[None, :]
    return jnp.concatenate([harmonic_fit[:split], harmonic_fit[split:] * land], 0)


def reference(year_slab, harmonic_fit, patterns, reader_table, land_mask):
    coeffs = effective(harmonic_fit, land_mask)
    blocks = year_slab.reshape(NCHUNK, TCH, P_SIZE)
    period = NCHUNK * TCH

    def one_block(pair):
        rows, group = pair
        hours = group * TCH + jnp.arange(TCH, dtype=jnp.int32)
        fitted = jnp.dot(regressors(hours, period), coeffs, precision=lax.Precision.HIGHEST)
        anomaly = (rows.astype(jnp.float32) - fitted).astype(jnp.bfloat16)
        return jnp.dot(anomaly, patterns, preferred_element_type=jnp.float32)

    result = lax.map(one_block, (blocks, reader_table))
    return result.reshape(NCHUNK * TCH, K)
```

```python
import functools
import math

import jax
import jax.numpy as jnp
from jax import lax
from jax.experimental import pallas as pl
from jax.experimental.pallas import tpu as pltpu
from jax.sharding import PartitionSpec as P

NHARM = 8
NDIUR = 2
SPLIT = 1 + 2 * NHARM
LANES = 4
F32 = jnp.float32
BF16 = jnp.bfloat16


def thirds(value):
    first = value.astype(BF16)
    rest = value - first.astype(F32)
    second = rest.astype(BF16)
    third = (rest - second.astype(F32)).astype(BF16)
    return first, second, third


def design_terms(hour, period):
    shape = (hour.shape[0], 128)
    lane = lax.broadcasted_iota(jnp.int32, shape, 1)
    j = lane & 31
    hour = jnp.broadcast_to(hour, shape)
    slow_sine = (j > NHARM).astype(jnp.int32)
    slow_order = j - NHARM * slow_sine
    slow = (hour * slow_order + slow_sine * (3 * period // 4)) & (period - 1)
    slow_angle = slow.astype(F32) * (2.0 * math.pi / period)
    i = j - SPLIT
    daily_sine = (i >= NDIUR).astype(jnp.int32)
    daily_order = i + 1 - NDIUR * daily_sine
    daily = (hour * daily_order + daily_sine * 18).astype(F32)
    daily = daily - 24.0 * jnp.floor((daily + 0.5) * (1.0 / 24.0))
    daily_angle = daily * (2.0 * math.pi / 24.0)
    angle = jnp.where(j == 0, 0.0, jnp.where(j < SPLIT, slow_angle, daily_angle))
    value = jnp.where(j < SPLIT + 2 * NDIUR, jnp.cos(angle), 0.0)
    first = value.astype(BF16).astype(F32)
    rest = value - first
    second = rest.astype(BF16).astype(F32)
    third = rest - second
    low = jnp.where(lane < 96, first, second)
    high = jnp.where(lane < 32, second, jnp.where(lane < 64, third, 0.0))
    return low.astype(BF16), high.astype(BF16)


def kernel(
    planes, table_ref, y_ref, c_ref, p_ref, mask_ref, out_ref,
    craw, mraw, cbuf, cstack, pbuf, ybuf, fit, design, sbuf, rbuf,
    local_sem, plane_send, plane_recv, y_send, y_recv, r_send, r_recv,
):
    rows, wide_columns = ybuf.shape[1:]
    columns = p_ref.shape[0]
    period = planes * LANES * rows
    me = lax.axis_index("wide")
    plane, lane = me // LANES, me % LANES
    side = me - lane + (lane + 2) % LANES
    core = me + 1 - 2 * (lane % 2)

    def at_plane(offset):
        return ((plane + offset + planes) % planes) * LANES + lane

    def block(which):
        return pl.ds(pl.multiple_of(which * columns, columns), columns)

    c_in = pltpu.make_async_copy(c_ref, craw, local_sem.at[0])
    m_in = pltpu.make_async_copy(mask_ref, mraw, local_sem.at[1])
    p_in = pltpu.make_async_copy(p_ref, pbuf.at[block(lane)], local_sem.at[2])
    here = pl.ds(pl.multiple_of(plane * wide_columns, wide_columns), wide_columns)
    y_in = pltpu.make_async_copy(y_ref.at[:, here], ybuf.at[0], local_sem.at[3])
    c_in.start()
    m_in.start()
    p_in.start()
    y_in.start()

    barrier = pltpu.get_barrier_semaphore()
    peers = [side, core] + [at_plane(d) for d in range(1, planes)]
    for peer in peers:
        pl.semaphore_signal(barrier, inc=1, device_id={"wide": peer}, device_id_type=pl.DeviceIdType.MESH)

    c_in.wait()
    m_in.wait()
    coeff_row = lax.broadcasted_iota(jnp.int32, craw.shape, 0)
    land = mraw[...].astype(F32)
    cbuf[lane] = jnp.zeros(cbuf.shape[1:], F32)
    cbuf[lane, 0:craw.shape[0], :] = craw[...] * jnp.where(coeff_row < SPLIT, 1.0, land)

    pl.semaphore_wait(barrier, len(peers))

    def remote(src, dst, send_sem, recv_sem, peer):
        return pltpu.make_async_remote_copy(
            src_ref=src, dst_ref=dst, send_sem=send_sem, recv_sem=recv_sem,
            device_id={"wide": peer}, device_id_type=pl.DeviceIdType.MESH,
        )

    p_side = remote(p_ref, pbuf.at[block(lane)], plane_send.at[0], plane_recv.at[0], side)
    c_side = remote(cbuf.at[lane], cbuf.at[lane], plane_send.at[1], plane_recv.at[1], side)
    p_core = remote(p_ref, pbuf.at[block(lane)], plane_send.at[2], plane_recv.at[2], core)
    c_core = remote(cbuf.at[lane], cbuf.at[lane], plane_send.at[3], plane_recv.at[3], core)
    other = (lane + 2) % LANES
    p_on = remote(pbuf.at[block(other)], pbuf.at[block(other)], plane_send.at[4], plane_recv.at[4], core)
    c_on = remote(cbuf.at[other], cbuf.at[other], plane_send.at[5], plane_recv.at[5], core)
    y_out = []
    for d in range(1, planes):
        to = (plane + d) % planes
        there = pl.ds(pl.multiple_of(to * wide_columns, wide_columns), wide_columns)
        y_out.append(remote(y_ref.at[:, there], ybuf.at[d], y_send.at[d], y_recv.at[d], at_plane(d)))
    c_side.start()
    for copy in y_out:
        copy.start()
    p_side.start()
    c_core.start()
    p_core.start()

    row = lax.broadcasted_iota(jnp.int32, (rows, 1), 0)
    for d in range(planes):
        hour = table_ref[at_plane(-d)] * rows + row
        low, high = design_terms(hour, period)
        design[d * rows:(d + 1) * rows, 0:128] = low
        design[d * rows:(d + 1) * rows, 128:256] = high
    cstack[...] = jnp.zeros(cstack.shape, BF16)

    c_side.wait_recv()
    c_on.start()
    c_core.wait_recv()
    p_side.wait_recv()
    p_on.start()
    c_on.wait_recv()
    zeros = jnp.zeros((8, columns), F32)
    for l in range(LANES):
        c1, c2, c3 = thirds(jnp.concatenate([cbuf[l], zeros], 0))
        at = slice(l * columns, (l + 1) * columns)
        for place, term in enumerate((c1, c2, c3, c1, c2, c1)):
            cstack[place * 32:(place + 1) * 32, at] = term
    fit[...] = jnp.dot(design[...], cstack[...], preferred_element_type=F32)

    p_in.wait()
    p_core.wait_recv()
    p_on.wait_recv()

    def project(d):
        anomaly = ybuf[d].astype(F32) - fit[d * rows:(d + 1) * rows, :]
        return jnp.dot(anomaly.astype(BF16), pbuf[...], preferred_element_type=F32)

    y_in.wait()
    total = project(0)
    r_out = []
    for d in range(1, planes):
        y_out[d - 1].wait_recv()
        sbuf[d] = project(d).astype(sbuf.dtype)
        copy = remote(sbuf.at[d], rbuf.at[d], r_send.at[d], r_recv.at[d], at_plane(-d))
        copy.start()
        r_out.append(copy)
    for d in range(1, planes):
        r_out[d - 1].wait_recv()
        total = total + rbuf[d].astype(F32)
    out_ref[...] = total
    for copy in [p_side, c_side, p_core, c_core, p_on, c_on] + y_out + r_out:
        copy.wait_send()


def local(year_slab, harmonic_fit, patterns, reader_table, land_mask):
    readers = lax.axis_size("wide")
    planes = readers // LANES
    rows = year_slab.shape[0]
    columns, patterns_held = patterns.shape
    wide_columns = LANES * columns
    hbm = pl.BlockSpec(memory_space=pl.ANY)
    return pl.pallas_call(
        functools.partial(kernel, planes),
        out_shape=jax.ShapeDtypeStruct((rows, patterns_held), F32),
        in_specs=[pl.BlockSpec(memory_space=pltpu.SMEM), hbm, hbm, hbm, hbm],
        out_specs=pl.BlockSpec(memory_space=pltpu.VMEM),
        scratch_shapes=[
            pltpu.VMEM(harmonic_fit.shape, F32),
            pltpu.VMEM((1, columns), jnp.int32),
            pltpu.VMEM((LANES, 24, columns), F32),
            pltpu.VMEM((256, wide_columns), BF16),
            pltpu.VMEM((wide_columns, patterns_held), BF16),
            pltpu.VMEM((planes, rows, wide_columns), BF16),
            pltpu.VMEM((planes * rows, wide_columns), F32),
            pltpu.VMEM((planes * rows, 256), BF16),
            pltpu.VMEM((planes, rows, patterns_held), BF16),
            pltpu.VMEM((planes, rows, patterns_held), BF16),
            pltpu.SemaphoreType.DMA((4,)),
            pltpu.SemaphoreType.DMA((6,)),
            pltpu.SemaphoreType.DMA((6,)),
            pltpu.SemaphoreType.DMA((planes,)),
            pltpu.SemaphoreType.DMA((planes,)),
            pltpu.SemaphoreType.DMA((planes,)),
            pltpu.SemaphoreType.DMA((planes,)),
        ],
        compiler_params=pltpu.CompilerParams(
            collective_id=0, has_side_effects=True, vmem_limit_bytes=63 * 1024 * 1024 + 900 * 1024
        ),
        cost_estimate=pl.CostEstimate(
            flops=2 * planes * rows * wide_columns * (patterns_held + 256),
            bytes_accessed=2 * rows * readers * columns + 2 * columns * patterns_held,
            transcendentals=0,
        ),
    )(reader_table, year_slab, harmonic_fit, patterns, land_mask.reshape(1, columns))


def solution(mesh):
    placed = (P(("grp", "wide"), None), P(None, "wide"), P("wide", None), P(), P("wide"))
    return jax.shard_map(
        local, mesh=mesh, in_specs=placed, out_specs=P(("grp", "wide"), None), check_vma=False
    )
```

```python
import functools
import math

import jax
import jax.numpy as jnp
from jax import lax
from jax.experimental import pallas as pl
from jax.experimental.pallas import tpu as pltpu
from jax.sharding import PartitionSpec as P

NHARM = 8
NDIUR = 2
SPLIT = 1 + 2 * NHARM
LANES = 4
F32 = jnp.float32
BF16 = jnp.bfloat16


def thirds(value):
    first = value.astype(BF16)
    rest = value - first.astype(F32)
    second = rest.astype(BF16)
    third = (rest - second.astype(F32)).astype(BF16)
    return first, second, third


def design_terms(hour, period):
    shape = (hour.shape[0], 128)
    lane = lax.broadcasted_iota(jnp.int32, shape, 1)
    j = lane & 31
    hour = jnp.broadcast_to(hour, shape)
    slow_sine = (j > NHARM).astype(jnp.int32)
    slow_order = j - NHARM * slow_sine
    slow = (hour * slow_order + slow_sine * (3 * period // 4)) & (period - 1)
    slow_angle = slow.astype(F32) * (2.0 * math.pi / period)
    i = j - SPLIT
    daily_sine = (i >= NDIUR).astype(jnp.int32)
    daily_order = i + 1 - NDIUR * daily_sine
    daily = (hour * daily_order + daily_sine * 18).astype(F32)
    daily = daily - 24.0 * jnp.floor((daily + 0.5) * (1.0 / 24.0))
    daily_angle = daily * (2.0 * math.pi / 24.0)
    angle = jnp.where(j == 0, 0.0, jnp.where(j < SPLIT, slow_angle, daily_angle))
    value = jnp.where(j < SPLIT + 2 * NDIUR, jnp.cos(angle), 0.0)
    first = value.astype(BF16).astype(F32)
    rest = value - first
    second = rest.astype(BF16).astype(F32)
    third = rest - second
    low = jnp.where(lane < 96, first, second)
    high = jnp.where(lane < 32, second, jnp.where(lane < 64, third, 0.0))
    return low.astype(BF16), high.astype(BF16)


def kernel(
    planes, table_hbm, y_ref, c_ref, p_ref, mask_ref, out_ref,
    table_ref, cbuf, mbuf, cpad, cstack, pbuf, ybuf, fit, design, sbuf, rbuf,
    local_sem, plane_send, plane_recv, y_send, y_recv, r_send, r_recv,
):
    rows, wide_columns = ybuf.shape[1:]
    columns = p_ref.shape[0]
    period = planes * LANES * rows
    me = lax.axis_index("wide")
    plane, lane = me // LANES, me % LANES
    side = me - lane + (lane + 2) % LANES
    core = me + 1 - 2 * (lane % 2)

    def at_plane(offset):
        return partner(offset) * LANES + lane

    def partner(offset):
        swapped, bit = plane, 1
        while bit < planes:
            if offset & bit:
                swapped = swapped + bit - 2 * bit * ((plane // bit) % 2)
            bit *= 2
        return swapped

    order = list(range(planes - 1, 0, -1))

    def block(which):
        return pl.ds(pl.multiple_of(which * columns, columns), columns)

    c_in = pltpu.make_async_copy(c_ref, cbuf.at[lane], local_sem.at[0])
    m_in = pltpu.make_async_copy(mask_ref, mbuf.at[lane], local_sem.at[1])
    p_in = pltpu.make_async_copy(p_ref, pbuf.at[block(lane)], local_sem.at[2])
    here = pl.ds(pl.multiple_of(plane * wide_columns, wide_columns), wide_columns)
    y_in = pltpu.make_async_copy(y_ref.at[:, here], ybuf.at[0], local_sem.at[3])
    t_in = pltpu.make_async_copy(table_hbm, table_ref, local_sem.at[4])
    t_in.start()
    c_in.start()
    m_in.start()
    p_in.start()
    y_in.start()

    barrier = pltpu.get_barrier_semaphore()
    peers = [side, core] + [at_plane(d) for d in range(1, planes)]
    for peer in peers:
        pl.semaphore_signal(barrier, inc=1, device_id={"wide": peer}, device_id_type=pl.DeviceIdType.MESH)

    pl.semaphore_wait(barrier, len(peers))

    def remote(src, dst, send_sem, recv_sem, peer):
        return pltpu.make_async_remote_copy(
            src_ref=src, dst_ref=dst, send_sem=send_sem, recv_sem=recv_sem,
            device_id={"wide": peer}, device_id_type=pl.DeviceIdType.MESH,
        )

    p_side = remote(p_ref, pbuf.at[block(lane)], plane_send.at[0], plane_recv.at[0], side)
    c_side = remote(c_ref, cbuf.at[lane], plane_send.at[1], plane_recv.at[1], side)
    m_side = remote(mask_ref, mbuf.at[lane], plane_send.at[6], plane_recv.at[6], side)
    p_core = remote(p_ref, pbuf.at[block(lane)], plane_send.at[2], plane_recv.at[2], core)
    c_core = remote(c_ref, cbuf.at[lane], plane_send.at[3], plane_recv.at[3], core)
    m_core = remote(mask_ref, mbuf.at[lane], plane_send.at[7], plane_recv.at[7], core)
    other = (lane + 2) % LANES
    p_on = remote(pbuf.at[block(other)], pbuf.at[block(other)], plane_send.at[4], plane_recv.at[4], core)
    c_on = remote(cbuf.at[other], cbuf.at[other], plane_send.at[5], plane_recv.at[5], core)
    m_on = remote(mbuf.at[other], mbuf.at[other], plane_send.at[8], plane_recv.at[8], core)
    y_out = {}
    for d in order:
        to = partner(d)
        there = pl.ds(pl.multiple_of(to * wide_columns, wide_columns), wide_columns)
        y_out[d] = remote(y_ref.at[:, there], ybuf.at[d], y_send.at[d], y_recv.at[d], at_plane(d))
    c_side.start()
    m_side.start()
    for copy in y_out.values():
        copy.start()
    p_side.start()
    c_core.start()
    m_core.start()
    p_core.start()

    row = lax.broadcasted_iota(jnp.int32, (rows, 1), 0)
    t_in.wait()
    for d in range(planes):
        hour = table_ref[at_plane(d)] * rows + row
        low, high = design_terms(hour, period)
        design[d * rows:(d + 1) * rows, 0:128] = low
        design[d * rows:(d + 1) * rows, 128:256] = high
    cstack[...] = jnp.zeros(cstack.shape, BF16)
    cpad[...] = jnp.zeros(cpad.shape, F32)
    held = cbuf.shape[1]
    masked = lax.broadcasted_iota(jnp.int32, cbuf.shape[1:], 0) >= SPLIT

    c_side.wait_recv()
    c_on.start()
    m_side.wait_recv()
    m_on.start()
    for copy in (c_in, m_in):
        copy.wait()
    for copy in (c_core, m_core, c_on, m_on):
        copy.wait_recv()
    for l in range(LANES):
        cpad[l, 0:held, :] = cbuf[l] * jnp.where(masked, mbuf[l].astype(F32), 1.0)
        c1, c2, c3 = thirds(cpad[l])
        at = slice(l * columns, (l + 1) * columns)
        for place, term in enumerate((c1, c2, c3, c1, c2, c1)):
            cstack[place * 32:(place + 1) * 32, at] = term
    fit[...] = jnp.dot(design[...], cstack[...], preferred_element_type=F32)

    p_side.wait_recv()
    p_on.start()
    p_in.wait()
    p_core.wait_recv()
    p_on.wait_recv()

    def project(d):
        anomaly = ybuf[d].astype(F32) - fit[d * rows:(d + 1) * rows, :]
        return jnp.dot(anomaly.astype(BF16), pbuf[...], preferred_element_type=F32)

    y_in.wait()
    total = project(0)
    r_out = {}
    for d in order:
        y_out[d].wait_recv()
        sbuf[d] = project(d).astype(sbuf.dtype)
        copy = remote(sbuf.at[d], rbuf.at[d], r_send.at[d], r_recv.at[d], at_plane(d))
        copy.start()
        r_out[d] = copy
    for d in order:
        r_out[d].wait_recv()
        total = total + rbuf[d].astype(F32)
    out_ref[...] = total
    for copy in [p_side, c_side, m_side, p_core, c_core, m_core, p_on, c_on, m_on] + list(y_out.values()) + list(r_out.values()):
        copy.wait_send()


def local(year_slab, harmonic_fit, patterns, reader_table, land_mask):
    readers = lax.axis_size("wide")
    planes = readers // LANES
    rows = year_slab.shape[0]
    columns, patterns_held = patterns.shape
    wide_columns = LANES * columns
    hbm = pl.BlockSpec(memory_space=pl.ANY)
    pin = functools.partial(pltpu.with_memory_space_constraint, memory_space=pltpu.HBM)
    return pl.pallas_call(
        functools.partial(kernel, planes),
        out_shape=jax.ShapeDtypeStruct((rows, patterns_held), F32),
        in_specs=[hbm] * 5,
        out_specs=pl.BlockSpec(memory_space=pltpu.VMEM),
        scratch_shapes=[
            pltpu.SMEM(reader_table.shape, jnp.int32),
            pltpu.VMEM((LANES,) + harmonic_fit.shape, F32),
            pltpu.VMEM((LANES, 1, columns), jnp.int32),
            pltpu.VMEM((LANES, 32, columns), F32),
            pltpu.VMEM((256, wide_columns), BF16),
            pltpu.VMEM((wide_columns, patterns_held), BF16),
            pltpu.VMEM((planes, rows, wide_columns), BF16),
            pltpu.VMEM((planes * rows, wide_columns), F32),
            pltpu.VMEM((planes * rows, 256), BF16),
            pltpu.VMEM((planes, rows, patterns_held), BF16),
            pltpu.VMEM((planes, rows, patterns_held), BF16),
            pltpu.SemaphoreType.DMA((5,)),
            pltpu.SemaphoreType.DMA((9,)),
            pltpu.SemaphoreType.DMA((9,)),
            pltpu.SemaphoreType.DMA((planes,)),
            pltpu.SemaphoreType.DMA((planes,)),
            pltpu.SemaphoreType.DMA((planes,)),
            pltpu.SemaphoreType.DMA((planes,)),
        ],
        compiler_params=pltpu.CompilerParams(
            collective_id=0, has_side_effects=True, vmem_limit_bytes=40 * 1024 * 1024
        ),
        cost_estimate=pl.CostEstimate(
            flops=2 * planes * rows * wide_columns * (patterns_held + 256),
            bytes_accessed=2 * rows * readers * columns + 2 * columns * patterns_held,
            transcendentals=0,
        ),
    )(pin(reader_table), pin(year_slab), pin(harmonic_fit), pin(patterns), pin(land_mask.reshape(1, columns)))


def solution(mesh):
    placed = (P(("grp", "wide"), None), P(None, "wide"), P("wide", None), P(), P("wide"))
    return jax.shard_map(
        local, mesh=mesh, in_specs=placed, out_specs=P(("grp", "wide"), None), check_vma=False
    )
```

```python
import functools
import math

import jax
import jax.numpy as jnp
from jax import lax
from jax.experimental import pallas as pl
from jax.experimental.pallas import tpu as pltpu
from jax.sharding import PartitionSpec as P

NHARM = 8
NDIUR = 2
SPLIT = 1 + 2 * NHARM
LANES = 4
F32 = jnp.float32
BF16 = jnp.bfloat16


def thirds(value):
    first = value.astype(BF16)
    rest = value - first.astype(F32)
    second = rest.astype(BF16)
    third = (rest - second.astype(F32)).astype(BF16)
    return first, second, third


def design_terms(hour, period):
    shape = (hour.shape[0], 128)
    lane = lax.broadcasted_iota(jnp.int32, shape, 1)
    j = lane & 31
    hour = jnp.broadcast_to(hour, shape)
    slow_sine = (j > NHARM).astype(jnp.int32)
    slow_order = j - NHARM * slow_sine
    slow = (hour * slow_order + slow_sine * (3 * period // 4)) & (period - 1)
    slow_angle = slow.astype(F32) * (2.0 * math.pi / period)
    i = j - SPLIT
    daily_sine = (i >= NDIUR).astype(jnp.int32)
    daily_order = i + 1 - NDIUR * daily_sine
    daily = (hour * daily_order + daily_sine * 18).astype(F32)
    daily = daily - 24.0 * jnp.floor((daily + 0.5) * (1.0 / 24.0))
    daily_angle = daily * (2.0 * math.pi / 24.0)
    angle = jnp.where(j == 0, 0.0, jnp.where(j < SPLIT, slow_angle, daily_angle))
    value = jnp.where(j < SPLIT + 2 * NDIUR, jnp.cos(angle), 0.0)
    first = value.astype(BF16).astype(F32)
    rest = value - first
    second = rest.astype(BF16).astype(F32)
    third = rest - second
    low = jnp.where(lane < 96, first, second)
    high = jnp.where(lane < 32, second, jnp.where(lane < 64, third, 0.0))
    return low.astype(BF16), high.astype(BF16)


def kernel(
    planes, table_hbm, y_ref, c_ref, p_ref, mask_ref, out_ref,
    table_ref, cbuf, mbuf, cpad, cstack, pbuf, ybuf, fit, design, sbuf, rbuf,
    local_sem, plane_send, plane_recv, y_send, y_recv, r_send, r_recv,
):
    rows, wide_columns = ybuf.shape[1:]
    columns = p_ref.shape[0]
    period = planes * LANES * rows
    me = lax.axis_index("wide")
    plane, lane = me // LANES, me % LANES
    side = me - lane + (lane + 2) % LANES
    core = me + 1 - 2 * (lane % 2)

    def at_plane(offset):
        return partner(offset) * LANES + lane

    def partner(offset):
        swapped, bit = plane, 1
        while bit < planes:
            if offset & bit:
                swapped = swapped + bit - 2 * bit * ((plane // bit) % 2)
            bit *= 2
        return swapped

    order = list(range(planes - 1, 0, -1))

    def block(which):
        return pl.ds(pl.multiple_of(which * columns, columns), columns)

    c_in = pltpu.make_async_copy(c_ref, cbuf.at[lane], local_sem.at[0])
    m_in = pltpu.make_async_copy(mask_ref, mbuf.at[lane], local_sem.at[1])
    p_in = pltpu.make_async_copy(p_ref, pbuf.at[block(lane)], local_sem.at[2])
    here = pl.ds(pl.multiple_of(plane * wide_columns, wide_columns), wide_columns)
    y_in = pltpu.make_async_copy(y_ref.at[:, here], ybuf.at[0], local_sem.at[3])
    t_in = pltpu.make_async_copy(table_hbm, table_ref, local_sem.at[4])
    t_in.start()
    c_in.start()
    m_in.start()
    p_in.start()
    y_in.start()

    barrier = pltpu.get_barrier_semaphore()
    peers = [side, core] + [at_plane(d) for d in range(1, planes)]
    for peer in peers:
        pl.semaphore_signal(barrier, inc=1, device_id={"wide": peer}, device_id_type=pl.DeviceIdType.MESH)

    pl.semaphore_wait(barrier, len(peers))

    def remote(src, dst, send_sem, recv_sem, peer):
        return pltpu.make_async_remote_copy(
            src_ref=src, dst_ref=dst, send_sem=send_sem, recv_sem=recv_sem,
            device_id={"wide": peer}, device_id_type=pl.DeviceIdType.MESH,
        )

    halves = [pl.ds(0, columns // 2), pl.ds(columns // 2, columns // 2)]

    def part(which, i):
        return pl.ds(pl.multiple_of(which * columns + i * (columns // 2), columns // 2), columns // 2)

    p_side = [remote(p_ref.at[halves[i]], pbuf.at[part(lane, i)], plane_send.at[(0, 9)[i]], plane_recv.at[(0, 9)[i]], side) for i in range(2)]
    c_side = remote(c_ref, cbuf.at[lane], plane_send.at[1], plane_recv.at[1], side)
    m_side = remote(mask_ref, mbuf.at[lane], plane_send.at[6], plane_recv.at[6], side)
    p_core = remote(p_ref, pbuf.at[block(lane)], plane_send.at[2], plane_recv.at[2], core)
    c_core = remote(c_ref, cbuf.at[lane], plane_send.at[3], plane_recv.at[3], core)
    m_core = remote(mask_ref, mbuf.at[lane], plane_send.at[7], plane_recv.at[7], core)
    other = (lane + 2) % LANES
    p_on = [remote(pbuf.at[part(other, i)], pbuf.at[part(other, i)], plane_send.at[(4, 10)[i]], plane_recv.at[(4, 10)[i]], core) for i in range(2)]
    c_on = remote(cbuf.at[other], cbuf.at[other], plane_send.at[5], plane_recv.at[5], core)
    m_on = remote(mbuf.at[other], mbuf.at[other], plane_send.at[8], plane_recv.at[8], core)
    y_out = {}
    for d in order:
        to = partner(d)
        there = pl.ds(pl.multiple_of(to * wide_columns, wide_columns), wide_columns)
        y_out[d] = remote(y_ref.at[:, there], ybuf.at[d], y_send.at[d], y_recv.at[d], at_plane(d))
    c_side.start()
    m_side.start()
    p_side[0].start()
    p_side[1].start()
    @pl.when(lane % 2 == 0)
    def _():
        for d in order:
            y_out[d].start()

    @pl.when(lane % 2 == 1)
    def _():
        for d in reversed(order):
            y_out[d].start()

    c_core.start()
    m_core.start()
    p_core.start()

    row = lax.broadcasted_iota(jnp.int32, (rows, 1), 0)
    t_in.wait()
    for d in range(planes):
        hour = table_ref[at_plane(d)] * rows + row
        low, high = design_terms(hour, period)
        design[d * rows:(d + 1) * rows, 0:128] = low
        design[d * rows:(d + 1) * rows, 128:192] = high[:, 0:64]
    cpad[...] = jnp.zeros(cpad.shape, F32)
    held = cbuf.shape[1]
    masked = lax.broadcasted_iota(jnp.int32, cbuf.shape[1:], 0) >= SPLIT

    c_side.wait_recv()
    c_on.start()
    m_side.wait_recv()
    m_on.start()
    for i in range(2):
        p_side[i].wait_recv()
        p_on[i].start()
    for copy in (c_in, m_in):
        copy.wait()
    for copy in (c_core, m_core, c_on, m_on):
        copy.wait_recv()
    for l in range(LANES):
        cpad[l, 0:held, :] = cbuf[l] * jnp.where(masked, mbuf[l].astype(F32), 1.0)
        c1, c2, c3 = thirds(cpad[l])
        at = slice(l * columns, (l + 1) * columns)
        for place, term in enumerate((c1, c2, c3, c1, c2, c1)):
            cstack[place * 32:(place + 1) * 32, at] = term
    fit[...] = jnp.dot(design[...], cstack[...], preferred_element_type=F32)

    p_in.wait()
    p_core.wait_recv()
    for copy in p_on:
        copy.wait_recv()

    def project(d):
        anomaly = ybuf[d].astype(F32) - fit[d * rows:(d + 1) * rows, :]
        return jnp.dot(anomaly.astype(BF16), pbuf[...], preferred_element_type=F32)

    y_in.wait()
    total = project(0)
    r_out = {}
    for d in order:
        y_out[d].wait_recv()
        sbuf[d] = project(d).astype(sbuf.dtype)
        copy = remote(sbuf.at[d], rbuf.at[d], r_send.at[d], r_recv.at[d], at_plane(d))
        copy.start()
        r_out[d] = copy
    for d in order:
        r_out[d].wait_recv()
        total = total + rbuf[d].astype(F32)
    out_ref[...] = total
    for copy in p_side + p_on + [c_side, m_side, p_core, c_core, m_core, c_on, m_on] + list(y_out.values()) + list(r_out.values()):
        copy.wait_send()


def local(year_slab, harmonic_fit, patterns, reader_table, land_mask):
    readers = lax.axis_size("wide")
    planes = readers // LANES
    rows = year_slab.shape[0]
    columns, patterns_held = patterns.shape
    wide_columns = LANES * columns
    hbm = pl.BlockSpec(memory_space=pl.ANY)
    pin = functools.partial(pltpu.with_memory_space_constraint, memory_space=pltpu.HBM)
    return pl.pallas_call(
        functools.partial(kernel, planes),
        out_shape=jax.ShapeDtypeStruct((rows, patterns_held), F32),
        in_specs=[hbm] * 5,
        out_specs=pl.BlockSpec(memory_space=pltpu.VMEM),
        scratch_shapes=[
            pltpu.SMEM(reader_table.shape, jnp.int32),
            pltpu.VMEM((LANES,) + harmonic_fit.shape, F32),
            pltpu.VMEM((LANES, 1, columns), jnp.int32),
            pltpu.VMEM((LANES, 32, columns), F32),
            pltpu.VMEM((192, wide_columns), BF16),
            pltpu.VMEM((wide_columns, patterns_held), BF16),
            pltpu.VMEM((planes, rows, wide_columns), BF16),
            pltpu.VMEM((planes * rows, wide_columns), F32),
            pltpu.VMEM((planes * rows, 192), BF16),
            pltpu.VMEM((planes, rows, patterns_held), BF16),
            pltpu.VMEM((planes, rows, patterns_held), BF16),
            pltpu.SemaphoreType.DMA((5,)),
            pltpu.SemaphoreType.DMA((11,)),
            pltpu.SemaphoreType.DMA((11,)),
            pltpu.SemaphoreType.DMA((planes,)),
            pltpu.SemaphoreType.DMA((planes,)),
            pltpu.SemaphoreType.DMA((planes,)),
            pltpu.SemaphoreType.DMA((planes,)),
        ],
        compiler_params=pltpu.CompilerParams(
            collective_id=0, has_side_effects=True, vmem_limit_bytes=40 * 1024 * 1024
        ),
        cost_estimate=pl.CostEstimate(
            flops=2 * planes * rows * wide_columns * (patterns_held + 256),
            bytes_accessed=2 * rows * readers * columns + 2 * columns * patterns_held,
            transcendentals=0,
        ),
    )(pin(reader_table), pin(year_slab), pin(harmonic_fit), pin(patterns), pin(land_mask.reshape(1, columns)))


def solution(mesh):
    placed = (P(("grp", "wide"), None), P(None, "wide"), P("wide", None), P(), P("wide"))
    return jax.shard_map(
        local, mesh=mesh, in_specs=placed, out_specs=P(("grp", "wide"), None), check_vma=False
    )
```

```python
import functools
import math

import jax
import jax.numpy as jnp
from jax import lax
from jax.experimental import pallas as pl
from jax.experimental.pallas import tpu as pltpu
from jax.sharding import PartitionSpec as P

NHARM = 8
NDIUR = 2
SPLIT = 1 + 2 * NHARM
LANES = 4
F32 = jnp.float32
BF16 = jnp.bfloat16


def thirds(value):
    first = value.astype(BF16)
    rest = value - first.astype(F32)
    second = rest.astype(BF16)
    third = (rest - second.astype(F32)).astype(BF16)
    return first, second, third


def design_terms(hour, period):
    shape = (hour.shape[0], 128)
    lane = lax.broadcasted_iota(jnp.int32, shape, 1)
    j = lane & 31
    hour = jnp.broadcast_to(hour, shape)
    slow_sine = (j > NHARM).astype(jnp.int32)
    slow_order = j - NHARM * slow_sine
    slow = (hour * slow_order + slow_sine * (3 * period // 4)) & (period - 1)
    slow_angle = slow.astype(F32) * (2.0 * math.pi / period)
    i = j - SPLIT
    daily_sine = (i >= NDIUR).astype(jnp.int32)
    daily_order = i + 1 - NDIUR * daily_sine
    daily = (hour * daily_order + daily_sine * 18).astype(F32)
    daily = daily - 24.0 * jnp.floor((daily + 0.5) * (1.0 / 24.0))
    daily_angle = daily * (2.0 * math.pi / 24.0)
    angle = jnp.where(j == 0, 0.0, jnp.where(j < SPLIT, slow_angle, daily_angle))
    value = jnp.where(j < SPLIT + 2 * NDIUR, jnp.cos(angle), 0.0)
    first = value.astype(BF16).astype(F32)
    rest = value - first
    second = rest.astype(BF16).astype(F32)
    third = rest - second
    low = jnp.where(lane < 96, first, second)
    high = jnp.where(lane < 32, second, jnp.where(lane < 64, third, 0.0))
    return low.astype(BF16), high.astype(BF16)


def kernel(
    planes, table_hbm, y_ref, c_ref, p_ref, mask_ref, out_ref,
    table_ref, cbuf, mbuf, cpad, cstack, pbuf, ybuf, fit, design, sbuf, rbuf,
    local_sem, plane_send, plane_recv, y_send, y_recv, r_send, r_recv,
):
    rows, wide_columns = ybuf.shape[1:]
    columns = p_ref.shape[0]
    period = planes * LANES * rows
    me = lax.axis_index("wide")
    plane, lane = me // LANES, me % LANES
    side = me - lane + (lane + 2) % LANES
    core = me + 1 - 2 * (lane % 2)

    def at_plane(offset):
        return partner(offset) * LANES + lane

    def partner(offset):
        swapped, bit = plane, 1
        while bit < planes:
            if offset & bit:
                swapped = swapped + bit - 2 * bit * ((plane // bit) % 2)
            bit *= 2
        return swapped

    order = list(range(planes - 1, 0, -1))

    def block(which):
        return pl.ds(pl.multiple_of(which * columns, columns), columns)

    c_in = pltpu.make_async_copy(c_ref, cbuf.at[lane], local_sem.at[0])
    m_in = pltpu.make_async_copy(mask_ref, mbuf.at[lane], local_sem.at[1])
    p_in = pltpu.make_async_copy(p_ref, pbuf.at[block(lane)], local_sem.at[2])
    here = pl.ds(pl.multiple_of(plane * wide_columns, wide_columns), wide_columns)
    y_in = pltpu.make_async_copy(y_ref.at[:, here], ybuf.at[0], local_sem.at[3])
    t_in = pltpu.make_async_copy(table_hbm, table_ref, local_sem.at[4])
    t_in.start()
    c_in.start()
    m_in.start()
    p_in.start()
    y_in.start()

    barrier = pltpu.get_barrier_semaphore()
    peers = [side, core] + [at_plane(d) for d in range(1, planes)]
    for peer in peers:
        pl.semaphore_signal(barrier, inc=1, device_id={"wide": peer}, device_id_type=pl.DeviceIdType.MESH)

    pl.semaphore_wait(barrier, len(peers))

    def remote(src, dst, send_sem, recv_sem, peer):
        return pltpu.make_async_remote_copy(
            src_ref=src, dst_ref=dst, send_sem=send_sem, recv_sem=recv_sem,
            device_id={"wide": peer}, device_id_type=pl.DeviceIdType.MESH,
        )

    halves = [pl.ds(0, columns // 2), pl.ds(columns // 2, columns // 2)]

    def part(which, i):
        return pl.ds(pl.multiple_of(which * columns + i * (columns // 2), columns // 2), columns // 2)

    p_side = [remote(p_ref.at[halves[i]], pbuf.at[part(lane, i)], plane_send.at[(0, 9)[i]], plane_recv.at[(0, 9)[i]], side) for i in range(2)]
    c_side = remote(c_ref, cbuf.at[lane], plane_send.at[1], plane_recv.at[1], side)
    m_side = remote(mask_ref, mbuf.at[lane], plane_send.at[6], plane_recv.at[6], side)
    p_core = remote(p_ref, pbuf.at[block(lane)], plane_send.at[2], plane_recv.at[2], core)
    c_core = remote(c_ref, cbuf.at[lane], plane_send.at[3], plane_recv.at[3], core)
    m_core = remote(mask_ref, mbuf.at[lane], plane_send.at[7], plane_recv.at[7], core)
    other = (lane + 2) % LANES
    p_on = [remote(pbuf.at[part(other, i)], pbuf.at[part(other, i)], plane_send.at[(4, 10)[i]], plane_recv.at[(4, 10)[i]], core) for i in range(2)]
    c_on = remote(cbuf.at[other], cbuf.at[other], plane_send.at[5], plane_recv.at[5], core)
    m_on = remote(mbuf.at[other], mbuf.at[other], plane_send.at[8], plane_recv.at[8], core)
    y_out = {}
    for d in order:
        to = partner(d)
        there = pl.ds(pl.multiple_of(to * wide_columns, wide_columns), wide_columns)
        y_out[d] = remote(y_ref.at[:, there], ybuf.at[d], y_send.at[d], y_recv.at[d], at_plane(d))
    c_side.start()
    m_side.start()
    p_side[0].start()
    p_side[1].start()
    @pl.when(lane % 2 == 0)
    def _():
        for d in order:
            y_out[d].start()

    @pl.when(lane % 2 == 1)
    def _():
        for d in reversed(order):
            y_out[d].start()

    c_core.start()
    m_core.start()
    p_core.start()

    row = lax.broadcasted_iota(jnp.int32, (rows, 1), 0)
    t_in.wait()
    for d in range(planes):
        hour = table_ref[at_plane(d)] * rows + row
        low, high = design_terms(hour, period)
        design[d * rows:(d + 1) * rows, 0:128] = low
        design[d * rows:(d + 1) * rows, 128:192] = high[:, 0:64]
    cpad[...] = jnp.zeros(cpad.shape, F32)
    held = cbuf.shape[1]
    masked = lax.broadcasted_iota(jnp.int32, cbuf.shape[1:], 0) >= SPLIT

    c_side.wait_recv()
    c_on.start()
    m_side.wait_recv()
    m_on.start()
    for i in range(2):
        p_side[i].wait_recv()
        p_on[i].start()
    for copy in (c_in, m_in):
        copy.wait()
    for copy in (c_core, m_core, c_on, m_on):
        copy.wait_recv()
    for l in range(LANES):
        cpad[l, 0:held, :] = cbuf[l] * jnp.where(masked, mbuf[l].astype(F32), 1.0)
        c1, c2, c3 = thirds(cpad[l])
        at = slice(l * columns, (l + 1) * columns)
        for place, term in enumerate((c1, c2, c3, c1, c2, c1)):
            cstack[place * 32:(place + 1) * 32, at] = term
    fit[...] = jnp.dot(design[...], cstack[...], preferred_element_type=F32)

    p_in.wait()
    p_core.wait_recv()
    for copy in p_on:
        copy.wait_recv()

    def project(d):
        anomaly = ybuf[d].astype(F32) - fit[d * rows:(d + 1) * rows, :]
        return jnp.dot(anomaly.astype(BF16), pbuf[...], preferred_element_type=F32)

    r_out = {}
    for d in order:
        y_out[d].wait_recv()
        sbuf[d] = project(d).astype(sbuf.dtype)
        copy = remote(sbuf.at[d], rbuf.at[d], r_send.at[d], r_recv.at[d], at_plane(d))
        copy.start()
        r_out[d] = copy
    y_in.wait()
    total = project(0)
    for d in order:
        r_out[d].wait_recv()
        total = total + rbuf[d].astype(F32)
    out_ref[...] = total
    for copy in p_side + p_on + [c_side, m_side, p_core, c_core, m_core, c_on, m_on] + list(y_out.values()) + list(r_out.values()):
        copy.wait_send()


def local(year_slab, harmonic_fit, patterns, reader_table, land_mask):
    readers = lax.axis_size("wide")
    planes = readers // LANES
    rows = year_slab.shape[0]
    columns, patterns_held = patterns.shape
    wide_columns = LANES * columns
    hbm = pl.BlockSpec(memory_space=pl.ANY)
    pin = functools.partial(pltpu.with_memory_space_constraint, memory_space=pltpu.HBM)
    return pl.pallas_call(
        functools.partial(kernel, planes),
        out_shape=jax.ShapeDtypeStruct((rows, patterns_held), F32),
        in_specs=[hbm] * 5,
        out_specs=pl.BlockSpec(memory_space=pltpu.VMEM),
        scratch_shapes=[
            pltpu.SMEM(reader_table.shape, jnp.int32),
            pltpu.VMEM((LANES,) + harmonic_fit.shape, F32),
            pltpu.VMEM((LANES, 1, columns), jnp.int32),
            pltpu.VMEM((LANES, 32, columns), F32),
            pltpu.VMEM((192, wide_columns), BF16),
            pltpu.VMEM((wide_columns, patterns_held), BF16),
            pltpu.VMEM((planes, rows, wide_columns), BF16),
            pltpu.VMEM((planes * rows, wide_columns), F32),
            pltpu.VMEM((planes * rows, 192), BF16),
            pltpu.VMEM((planes, rows, patterns_held), BF16),
            pltpu.VMEM((planes, rows, patterns_held), BF16),
            pltpu.SemaphoreType.DMA((5,)),
            pltpu.SemaphoreType.DMA((11,)),
            pltpu.SemaphoreType.DMA((11,)),
            pltpu.SemaphoreType.DMA((planes,)),
            pltpu.SemaphoreType.DMA((planes,)),
            pltpu.SemaphoreType.DMA((planes,)),
            pltpu.SemaphoreType.DMA((planes,)),
        ],
        compiler_params=pltpu.CompilerParams(
            collective_id=0, has_side_effects=True, vmem_limit_bytes=40 * 1024 * 1024
        ),
        cost_estimate=pl.CostEstimate(
            flops=2 * planes * rows * wide_columns * (patterns_held + 256),
            bytes_accessed=2 * rows * readers * columns + 2 * columns * patterns_held,
            transcendentals=0,
        ),
    )(pin(reader_table), pin(year_slab), pin(harmonic_fit), pin(patterns), pin(land_mask.reshape(1, columns)))


def solution(mesh):
    placed = (P(("grp", "wide"), None), P(None, "wide"), P("wide", None), P(), P("wide"))
    return jax.shard_map(
        local, mesh=mesh, in_specs=placed, out_specs=P(("grp", "wide"), None), check_vma=False
    )
```
